32 devices in a mesh: dp: 8 (over z, y), mp: 4 (over x, core).
Axes of the slice: x: 2, y: 2, z: 4, core: 2. Of those that a mesh axis runs over, the one named last changes fastest.
Arguments:
- statistics: float32 [384, 256, 256], P(('dp', 'mp')), may hold values from -6 to 40, as said below
- gradient: float32 [192, 256, 256], P('dp', 'mp'), may hold values from -6 to 6
- root_table: int32 [4, 96], P('mp'), may hold values from 0 to 7, as said below
Outputs:
- root_store: float32 [768, 256, 256], P(('dp', 'mp'))
- update: float32 [192, 256, 256], P('dp', 'mp')
The draws below stay inside these ranges and needn't reach their ends.
Inputs may be any that keep to these rules, and one draw needn't show every extreme that they name: `statistics`: every block is symmetric and positive definite. `root_table`: in each row no worker is named more than 24 times and some worker exactly 24 times; the 12 entries of one dp index name no worker more than 3 times, and in each row some dp index names one worker exactly 3 times.
All inputs are finite; a program needn't handle non-finite values.
Results may differ from the reference program's by a relative error of at most 0.00022.
Values sent between devices are 32-bit elements; how exact they have to be, the bound alone decides.
A program may use at most 128 MiB of HBM per device.

```python
import math
import jax
import jax.numpy as jnp
from jax import lax

BLOCK = 256
FAC_DEV = 12
ITERS = 3
CAP = 24
BLOCKS = 192
N_DP = 8
N_MP = 4


def draw_statistics(key, part):
    key = jax.random.fold_in(key, 5)
    key_diag, key_rough = jax.random.split(key)
    count = N_DP * N_MP * FAC_DEV
    spread = 0.72 / math.sqrt(BLOCK)
    lowest, highest = (1.0, 10.0)
    diagonal = jnp.exp(jax.random.uniform(key_diag, (count, BLOCK), jnp.float32, math.log(lowest), math.log(highest)))
    rough = jax.random.uniform(key_rough, (count, BLOCK, BLOCK), jnp.float32, -spread, spread)
    rough = (rough + jnp.swapaxes(rough, 1, 2)) * 0.5
    identity = jnp.eye(BLOCK, dtype=jnp.float32)
    rooted = jnp.sqrt(diagonal)
    return (rooted[:, :, None] * rooted[:, None, :] * (rough * (1.0 - identity) + identity)).astype(jnp.float32)


def draw_root_table(key, part):
    key = jax.random.fold_in(key, 11)
    columns = []
    for column in range(N_MP):
        column_key = jax.random.fold_in(key, column)
        key_perm, key_delta, key_shift = jax.random.split(column_key, 3)
        order = jax.random.permutation(key_perm, N_DP)
        deltas = jax.random.randint(key_delta, (N_DP // 2,), 0, FAC_DEV + 1)
        deltas = deltas.at[0].set(FAC_DEV)
        loads = jnp.zeros((N_DP,), jnp.int32)
        loads = loads.at[order[0::2]].set(FAC_DEV + deltas).at[order[1::2]].set(FAC_DEV - deltas)
        bounds = jnp.cumsum(loads)
        entries = jnp.arange(N_DP * FAC_DEV, dtype=jnp.int32)
        owners = jnp.sum((entries[:, None] >= bounds[None, :]).astype(jnp.int32), axis=1)
        rotation = jax.random.randint(key_shift, (), 0, N_DP)
        sources = (entries + rotation) % N_DP
        positions = sources * FAC_DEV + entries // N_DP
        column_row = jnp.zeros((N_DP * FAC_DEV,), jnp.int32).at[positions].set(owners)
        columns.append(column_row)
    return jnp.stack(columns).astype(jnp.int32)


def steps_of(key, shape, cuts, least, high):
    factor_of = 1.0
    for dim, blocks in cuts:
        steps = jax.random.uniform(jax.random.fold_in(jax.random.fold_in(key, 6), dim), (blocks,), jnp.float32, least / len(cuts), high / len(cuts))
        factor_of = factor_of * jnp.repeat(jnp.exp(steps), shape[dim] // blocks).reshape((-1,) + (1,) * (len(shape) - 1 - dim))
    return factor_of


def normal_values(stream_key, extent, width, reach, cuts=(), kind=jnp.bfloat16):
    values = jax.random.normal(stream_key, extent, jnp.float32) * width
    if len(cuts) > 0:
        values = steps_of(stream_key, extent, cuts, -0.22, 0.18) * values
    return jnp.clip(values, min=-reach, max=reach).astype(kind)


def setup_inputs(seed: int = 0) -> dict:
    seeds = jax.random.split(jax.random.key(seed), 4)
    statistics = draw_statistics(jax.random.fold_in(seeds[3], 71), 0)
    gradient = normal_values(seeds[1], (BLOCKS, BLOCK, BLOCK), 1.0, 6.0, ((0, 8), (1, 4)), jnp.float32)
    root_table = draw_root_table(jax.random.fold_in(seeds[3], 71), 0)
    return {"statistics": statistics, "gradient": gradient, "root_table": root_table}


def product(left, right):
    return jnp.dot(left, right, precision=lax.Precision.HIGHEST, preferred_element_type=jnp.float32)

def inverse_root(statistic):
    identity = jnp.eye(BLOCK, dtype=jnp.float32)
    frob_scale = jnp.sqrt(jnp.sum(statistic * statistic) + 1e-06)
    quarter = 1.0 / jnp.sqrt(jnp.sqrt(frob_scale))
    moment = statistic / frob_scale
    root_now = identity
    for iteration in range(ITERS):
        newton_step = (5.0 * identity - moment) * 0.25
        if iteration == 0:
            root_now = quarter * newton_step
        else:
            root_now = product(root_now, newton_step)
        if iteration + 1 < ITERS:
            square = product(newton_step, newton_step)
            moment = product(product(square, square), moment)
    return root_now

def column_slots(targets):
    workers = jnp.arange(N_DP, dtype=jnp.int32)
    onehot = (targets[:, None] == workers[None, :]).astype(jnp.int32)
    before = jnp.cumsum(onehot, axis=0) - onehot
    return lax.optimization_barrier(jnp.sum(before * onehot, axis=1)).astype(jnp.int32)

def precondition(block_item):
    grad_block, pair_roots = block_item
    return product(product(pair_roots[0], grad_block), pair_roots[1])

def reference(statistics, gradient, root_table):
    inverse_roots = lax.map(inverse_root, statistics)
    workers = jnp.arange(N_DP, dtype=jnp.int32)
    factor_ids = jnp.arange(N_DP * FAC_DEV, dtype=jnp.int32)
    slot_ids = jnp.arange(CAP, dtype=jnp.int32)
    chosen_rows = []
    occupied = []
    for column in range(N_MP):
        targets = root_table[column].astype(jnp.int32)
        worker_slots = column_slots(targets)
        matches = (targets[:, None, None] == workers[None, :, None]) & (worker_slots[:, None, None] == slot_ids[None, None, :])
        chosen = lax.optimization_barrier(jnp.sum(matches.astype(jnp.int32) * factor_ids[:, None, None], axis=0)).astype(jnp.int32)
        factor_rows = (chosen // FAC_DEV * N_MP + column) * FAC_DEV + chosen % FAC_DEV
        chosen_rows.append(factor_rows.astype(jnp.int32))
        occupied.append(jnp.any(matches, axis=0))
    chosen_rows = jnp.stack(chosen_rows, axis=1).reshape(-1)
    occupied = jnp.stack(occupied, axis=1).reshape(-1)
    root_store = jnp.where(occupied[:, None, None], inverse_roots[chosen_rows], jnp.zeros((), jnp.float32))
    root_pairs = inverse_roots.reshape(BLOCKS, 2, BLOCK, BLOCK)
    update = lax.map(precondition, (gradient, root_pairs))
    return (root_store, update)
```

```python
import functools

import jax
import jax.numpy as jnp
from jax import lax
from jax.experimental import pallas as pl
from jax.experimental.pallas import tpu as pltpu
from jax.sharding import PartitionSpec as P

MESH = pl.DeviceIdType.MESH
F32 = jnp.float32
BF16 = jnp.bfloat16


def one_pass(left, right):
    return jnp.dot(left.astype(BF16), right.astype(BF16), preferred_element_type=F32)


def halves(value):
    high = value.astype(BF16)
    return high, (value - high.astype(F32)).astype(BF16)


def three_pass(left, right):
    left_high, left_low = halves(left)
    right_high, right_low = halves(right)
    dot = functools.partial(jnp.dot, preferred_element_type=F32)
    return dot(left_high, right_high) + (dot(left_high, right_low) + dot(left_low, right_high))


def inverse_root(stat, eye_mask):
    scale = jnp.sqrt(jnp.sum(stat * stat, keepdims=True) + 1e-06)
    quarter = 1.0 / jnp.sqrt(jnp.sqrt(scale))
    x = stat * (-0.25 / scale)
    c = 1.5625
    xx = one_pass(x, x)
    a = 2.5 * x + xx
    b = 3.125 * a + one_pass(a, a)
    d = 1.25 * x + xx
    y = 1.25 * x + (c * c) * d + one_pass(b, d)
    z = (2 * c) * y + one_pass(y, y)
    w = (2 * c * c) * z + one_pass(z, z)
    t = c * x + one_pass(x, y)
    e = 1.25 * y + (c**4) * t + three_pass(w, t)
    return quarter * jnp.where(eye_mask, e + 1.25 * c, e)


def shifts(count):
    return sorted(range(1, count), key=lambda k: abs(k - count / 2))


def spread_kernel(
    dp_count,
    mp_count,
    per_peer,
    group,
    table_ref,
    stat_ref,
    grad_ref,
    recv_ref,
    back_ref,
    roots,
    packed,
    corner,
    staged,
    whole,
    result,
    grad_send,
    grad_recv,
    back_send,
    back_recv,
    out_send,
    out_recv,
    local_sem,
):
    dp_me = lax.axis_index("dp")
    mp_me = lax.axis_index("mp")
    factors, width = stat_ref.shape[0], stat_ref.shape[1]
    half = width // 2
    pairs = factors // 2
    rows = width // mp_count
    barrier = pltpu.get_barrier_semaphore()
    for k in range(1, dp_count):
        pl.semaphore_signal(
            barrier, inc=1, device_id=(lax.rem(dp_me + k, dp_count), mp_me), device_id_type=MESH
        )
    for j in range(1, mp_count):
        pl.semaphore_signal(
            barrier, inc=1, device_id=(dp_me, lax.rem(mp_me + j, mp_count)), device_id_type=MESH
        )
    pl.semaphore_wait(barrier, dp_count + mp_count - 2)

    my_rows = pl.ds(pl.multiple_of(mp_me * rows, rows), rows)
    grad_copies = []
    for j in range(1, mp_count):
        peer = lax.rem(mp_me + j, mp_count)
        copy = pltpu.make_async_remote_copy(
            src_ref=grad_ref.at[pl.ds(peer * pairs, pairs)],
            dst_ref=whole.at[:, my_rows, :],
            send_sem=grad_send.at[j - 1],
            recv_sem=grad_recv.at[j - 1],
            device_id=(dp_me, peer),
            device_id_type=MESH,
        )
        copy.start()
        grad_copies.append(copy)
    own_grad = pltpu.make_async_copy(
        grad_ref.at[pl.ds(mp_me * pairs, pairs)], whole.at[:, my_rows, :], local_sem.at[0]
    )
    own_grad.start()

    down = lax.broadcasted_iota(jnp.int32, (half, half), 0)
    across = lax.broadcasted_iota(jnp.int32, (half, half), 1)
    eye_mask = lax.broadcasted_iota(jnp.int32, (width, width), 0) == lax.broadcasted_iota(
        jnp.int32, (width, width), 1
    )

    def make_roots(step, carry):
        for i in range(group):
            f = step * group + i
            root = inverse_root(stat_ref[f], eye_mask)
            roots[f] = root
            low = root[half:, half:]
            packed[f, :half, :] = root[half:, :half]
            packed[f, half:, :] = jnp.where(down >= across, root[:half, :half], low)
            diagonal = jnp.sum(jnp.where(down == across, low, 0.0), axis=0, keepdims=True)
            corner[f] = jnp.broadcast_to(diagonal, (8, half))
        return carry

    lax.fori_loop(0, factors // group, make_roots, 0)

    body = per_peer * width
    copies = []
    for k in shifts(dp_count) + [0]:
        peer = lax.rem(dp_me + k, dp_count)
        picks = [jnp.int32(0)] * per_peer
        filled = jnp.int32(0)
        base = dp_me * factors
        for f in range(factors):
            hit = table_ref[0, base + f] == peer
            for c in range(per_peer):
                picks[c] = jnp.where(jnp.logical_and(hit, filled == c), f, picks[c])
            filled = filled + hit.astype(jnp.int32)
        for c in range(per_peer):
            staged[k, c * width : (c + 1) * width, :] = packed[picks[c]]
            staged[k, body + 8 * c : body + 8 * c + 8, :] = corner[picks[c]]
        if k:
            copy = pltpu.make_async_remote_copy(
                src_ref=staged.at[k],
                dst_ref=recv_ref.at[dp_me],
                send_sem=out_send.at[k - 1],
                recv_sem=out_recv.at[k - 1],
                device_id=(peer, mp_me),
                device_id_type=MESH,
            )
            copy.start()
            copies.append(copy)
    own_roots = pltpu.make_async_copy(staged.at[0], recv_ref.at[dp_me], local_sem.at[1])
    own_roots.start()

    own_grad.wait()
    for copy in grad_copies:
        copy.wait()

    def apply(m, carry):
        left = three_pass(roots[2 * m], whole[m])
        result[m] = three_pass(left, roots[2 * m + 1])
        return carry

    lax.fori_loop(0, pairs, apply, 0)

    back_copies = []
    for j in range(1, mp_count):
        peer = lax.rem(mp_me + j, mp_count)
        copy = pltpu.make_async_remote_copy(
            src_ref=result.at[:, pl.ds(pl.multiple_of(peer * rows, rows), rows), :],
            dst_ref=back_ref.at[pl.ds(mp_me * pairs, pairs)],
            send_sem=back_send.at[j - 1],
            recv_sem=back_recv.at[j - 1],
            device_id=(dp_me, peer),
            device_id_type=MESH,
        )
        copy.start()
        back_copies.append(copy)
    own_back = pltpu.make_async_copy(
        result.at[:, my_rows, :], back_ref.at[pl.ds(mp_me * pairs, pairs)], local_sem.at[2]
    )
    own_back.start()
    own_back.wait()
    own_roots.wait()
    for copy in back_copies:
        copy.wait()
    for copy in copies:
        copy.wait()


def store_kernel(
    dp_count,
    per_peer,
    factors,
    per_step,
    table_ref,
    recv_ref,
    back_ref,
    store_ref,
    update_ref,
    sources,
    places,
    update_sem,
):
    step = pl.program_id(0)
    me = lax.axis_index("dp")
    half = store_ref.shape[2] // 2
    capacity = 2 * factors
    update_copy = pltpu.make_async_copy(back_ref, update_ref, update_sem)

    @pl.when(step == 0)
    def _():
        update_copy.start()
        for c in range(capacity + 1):
            sources[c] = -1
            places[c] = 0

        def from_source(source, slot):
            place = jnp.int32(0)
            for f in range(factors):
                hit = (table_ref[0, source * factors + f] == me).astype(jnp.int32)
                at = jnp.where(hit == 1, jnp.minimum(slot, capacity), capacity)
                sources[at] = source
                places[at] = place
                place = jnp.minimum(place + hit, per_peer - 1)
                slot = slot + hit
            return slot

        lax.fori_loop(0, dp_count, from_source, jnp.int32(0))

    down = lax.broadcasted_iota(jnp.int32, (half, half), 0)
    across = lax.broadcasted_iota(jnp.int32, (half, half), 1)
    body = per_peer * 2 * half
    for i in range(per_step):
        slot = step * per_step + i
        taken = sources[slot] >= 0
        source = jnp.maximum(sources[slot], 0)
        place = places[slot]
        first = pl.multiple_of(place * 2 * half, 2 * half)
        cross = recv_ref[source, pl.ds(first, half), :]
        mixed = recv_ref[source, pl.ds(pl.multiple_of(first + half, half), half), :]
        corner = recv_ref[source, pl.ds(pl.multiple_of(body + 8 * place, 8), 8), :][:1]
        cross = jnp.where(taken, cross, 0.0)
        mixed = jnp.where(taken, mixed, 0.0)
        corner = jnp.where(taken, corner, 0.0)
        turned = mixed.T
        store_ref[i, :half, :half] = jnp.where(down >= across, mixed, turned)
        store_ref[i, :half, half:] = cross.T
        store_ref[i, half:, :half] = cross
        store_ref[i, half:, half:] = jnp.where(
            down < across, mixed, jnp.where(down == across, corner, turned)
        )

    @pl.when(step == pl.num_programs(0) - 1)
    def _():
        update_copy.wait()


def on_device(statistics, gradient, root_table):
    dp_count = lax.axis_size("dp")
    mp_count = lax.axis_size("mp")
    factors, width = statistics.shape[0], statistics.shape[1]
    half, pairs = width // 2, factors // 2
    per_peer = (2 * factors + dp_count - 1) // dp_count
    group = 2 if factors % 2 == 0 else 1
    length = per_peer * (width + 8)
    table_spec = pl.BlockSpec(memory_space=pltpu.SMEM)
    any_spec = pl.BlockSpec(memory_space=pl.ANY)
    vmem_spec = pl.BlockSpec(memory_space=pltpu.VMEM)
    received, back = pl.pallas_call(
        functools.partial(spread_kernel, dp_count, mp_count, per_peer, group),
        out_shape=(
            jax.ShapeDtypeStruct((dp_count, length, half), F32),
            jax.ShapeDtypeStruct(gradient.shape, F32),
        ),
        in_specs=[table_spec, vmem_spec, any_spec],
        out_specs=(any_spec, any_spec),
        scratch_shapes=[
            pltpu.VMEM((factors, width, width), F32),
            pltpu.VMEM((factors, width, half), F32),
            pltpu.VMEM((factors, 8, half), F32),
            pltpu.VMEM((dp_count, length, half), F32),
            pltpu.VMEM((pairs, width, width), F32),
            pltpu.VMEM((pairs, width, width), F32),
            pltpu.SemaphoreType.DMA((mp_count - 1,)),
            pltpu.SemaphoreType.DMA((mp_count - 1,)),
            pltpu.SemaphoreType.DMA((mp_count - 1,)),
            pltpu.SemaphoreType.DMA((mp_count - 1,)),
            pltpu.SemaphoreType.DMA((dp_count - 1,)),
            pltpu.SemaphoreType.DMA((dp_count - 1,)),
            pltpu.SemaphoreType.DMA((3,)),
        ],
        compiler_params=pltpu.CompilerParams(
            collective_id=0, has_side_effects=True, vmem_limit_bytes=48 * 2**20
        ),
    )(root_table, statistics, gradient)
    per_step = 2
    capacity = 2 * factors
    return pl.pallas_call(
        functools.partial(store_kernel, dp_count, per_peer, factors, per_step),
        grid=(capacity // per_step,),
        out_shape=(
            jax.ShapeDtypeStruct((capacity, width, width), F32),
            jax.ShapeDtypeStruct(gradient.shape, F32),
        ),
        in_specs=[table_spec, vmem_spec, any_spec],
        out_specs=(pl.BlockSpec((per_step, width, width), lambda s: (s, 0, 0)), any_spec),
        scratch_shapes=[
            pltpu.SMEM((capacity + 1,), jnp.int32),
            pltpu.SMEM((capacity + 1,), jnp.int32),
            pltpu.SemaphoreType.DMA,
        ],
        compiler_params=pltpu.CompilerParams(vmem_limit_bytes=32 * 2**20),
    )(root_table, received, back)


def solution(mesh):
    return jax.shard_map(
        on_device,
        mesh=mesh,
        in_specs=(P(("dp", "mp"), None, None), P("dp", "mp", None), P("mp", None)),
        out_specs=(P(("dp", "mp"), None, None), P("dp", "mp", None)),
        check_vma=False,
    )
```

```python
import functools

import jax
import jax.numpy as jnp
from jax import lax
from jax.experimental import pallas as pl
from jax.experimental.pallas import tpu as pltpu
from jax.sharding import PartitionSpec as P

MESH = pl.DeviceIdType.MESH
F32 = jnp.float32
BF16 = jnp.bfloat16


def one_pass(left, right):
    return jnp.dot(left.astype(BF16), right.astype(BF16), preferred_element_type=F32)


def halves(value):
    high = value.astype(BF16)
    return high, (value - high.astype(F32)).astype(BF16)


def three_pass(left, right):
    left_high, left_low = halves(left)
    right_high, right_low = halves(right)
    dot = functools.partial(jnp.dot, preferred_element_type=F32)
    return dot(left_high, right_high) + (dot(left_high, right_low) + dot(left_low, right_high))


def inverse_root(stat, eye_mask):
    scale = jnp.sqrt(jnp.sum(stat * stat, keepdims=True) + 1e-06)
    quarter = 1.0 / jnp.sqrt(jnp.sqrt(scale))
    x = stat * (-0.25 / scale)
    c = 1.5625
    xx = one_pass(x, x)
    a = 2.5 * x + xx
    b = 3.125 * a + one_pass(a, a)
    d = 1.25 * x + xx
    y = 1.25 * x + (c * c) * d + one_pass(b, d)
    z = (2 * c) * y + one_pass(y, y)
    w = (2 * c * c) * z + one_pass(z, z)
    t = c * x + one_pass(x, y)
    e = 1.25 * y + (c**4) * t + three_pass(w, t)
    return quarter * jnp.where(eye_mask, e + 1.25 * c, e)


def flipped(me, mask, count):
    peer = me
    bit = 1
    while bit < count:
        peer = peer + (mask // bit % 2) * (1 - 2 * (me // bit % 2)) * bit
        bit *= 2
    return peer


def spread_kernel(
    dp_count,
    mp_count,
    per_peer,
    table_ref,
    stat_ref,
    grad_ref,
    recv_ref,
    back_ref,
    codes_ref,
    stats,
    roots,
    packed,
    corner,
    staged,
    whole,
    result,
    order,
    position,
    bases,
    grad_send,
    grad_recv,
    back_send,
    back_recv,
    out_send,
    out_recv,
    local_sem,
):
    dp_me = lax.axis_index("dp")
    mp_me = lax.axis_index("mp")
    factors, width = stats.shape[0], stats.shape[1]
    half = width // 2
    pairs = factors // 2
    rows = width // mp_count
    stat_copy = pltpu.make_async_copy(stat_ref, stats, local_sem.at[3])
    stat_copy.start()
    my_rows = pl.ds(pl.multiple_of(mp_me * rows, rows), rows)
    own_grad = pltpu.make_async_copy(
        grad_ref.at[pl.ds(mp_me * pairs, pairs)], whole.at[:, my_rows, :], local_sem.at[0]
    )
    own_grad.start()
    barrier = pltpu.get_barrier_semaphore()
    for k in range(1, dp_count):
        pl.semaphore_signal(
            barrier, inc=1, device_id=(lax.rem(dp_me + k, dp_count), mp_me), device_id_type=MESH
        )
    for j in range(1, mp_count):
        pl.semaphore_signal(
            barrier, inc=1, device_id=(dp_me, lax.rem(mp_me + j, mp_count)), device_id_type=MESH
        )

    targets = [table_ref[0, dp_me * factors + f] for f in range(factors)]
    places = [jnp.int32(0)] * factors
    running = jnp.int32(0)
    for s in range(dp_count):
        peer = flipped(dp_me, dp_count - 1 - s, dp_count)
        bases[s] = running
        for f in range(factors):
            hit = targets[f] == peer
            places[f] = jnp.where(hit, running, places[f])
            running = running + hit.astype(jnp.int32)
    for f in range(factors):
        position[f] = places[f]
    for i in range(factors):
        which = jnp.int32(0)
        for f in range(factors):
            which = jnp.where(places[f] == i, f, which)
        order[i] = which

    pl.semaphore_wait(barrier, dp_count + mp_count - 2)
    grad_copies = []
    for j in range(1, mp_count):
        peer = lax.rem(mp_me + j, mp_count)
        copy = pltpu.make_async_remote_copy(
            src_ref=grad_ref.at[pl.ds(peer * pairs, pairs)],
            dst_ref=whole.at[:, my_rows, :],
            send_sem=grad_send.at[j - 1],
            recv_sem=grad_recv.at[j - 1],
            device_id=(dp_me, peer),
            device_id_type=MESH,
        )
        copy.start()
        grad_copies.append(copy)

    down = lax.broadcasted_iota(jnp.int32, (half, half), 0)
    across = lax.broadcasted_iota(jnp.int32, (half, half), 1)
    eye_mask = lax.broadcasted_iota(jnp.int32, (width, width), 0) == lax.broadcasted_iota(
        jnp.int32, (width, width), 1
    )
    body = per_peer * width
    tail = staged.shape[1] - body
    tail_row = lax.broadcasted_iota(jnp.int32, (tail, half), 0)

    def stage(s):
        corners = jnp.zeros((tail, half), F32)
        for c in range(per_peer):
            at = jnp.minimum(bases[s] + c, factors - 1)
            staged[s, c * width : (c + 1) * width, :] = packed[at]
            corners = jnp.where(tail_row == c, corner[at][:1], corners)
        staged[s, body:, :] = corners

    def send(s):
        return pltpu.make_async_remote_copy(
            src_ref=staged.at[s],
            dst_ref=recv_ref.at[dp_me],
            send_sem=out_send.at[s],
            recv_sem=out_recv.at[s],
            device_id=(flipped(dp_me, dp_count - 1 - s, dp_count), mp_me),
            device_id_type=MESH,
        )

    stat_copy.wait()
    steps = factors // per_peer

    def make_roots(step, carry):
        for i in range(per_peer):
            f = step * per_peer + i
            root = inverse_root(stats[order[f]], eye_mask)
            roots[f] = root
            low = root[half:, half:]
            packed[f, :half, :] = root[half:, :half]
            packed[f, half:, :] = jnp.where(down >= across, root[:half, :half], low)
            diagonal = jnp.sum(jnp.where(down == across, low, 0.0), axis=0, keepdims=True)
            corner[f] = jnp.broadcast_to(diagonal, (8, half))
        stage(step)
        send(step).start()
        return carry

    def send_rest(s, carry):
        stage(s)
        send(s).start()
        return carry

    for f in range(factors):
        packed[f] = jnp.zeros((width, half), F32)
        corner[f] = jnp.zeros((8, half), F32)
    lax.fori_loop(0, steps, make_roots, 0)
    lax.fori_loop(steps, dp_count - 1, send_rest, 0)
    stage(dp_count - 1)
    own_roots = pltpu.make_async_copy(
        staged.at[dp_count - 1], recv_ref.at[dp_me], local_sem.at[1]
    )
    own_roots.start()

    own_grad.wait()
    for copy in grad_copies:
        copy.wait()

    def apply(m, carry):
        left = three_pass(roots[position[2 * m]], whole[m])
        result[m] = three_pass(left, roots[position[2 * m + 1]])
        return carry

    lax.fori_loop(0, pairs, apply, 0)

    back_copies = []
    for j in range(1, mp_count):
        peer = lax.rem(mp_me + j, mp_count)
        copy = pltpu.make_async_remote_copy(
            src_ref=result.at[:, pl.ds(pl.multiple_of(peer * rows, rows), rows), :],
            dst_ref=back_ref.at[pl.ds(mp_me * pairs, pairs)],
            send_sem=back_send.at[j - 1],
            recv_sem=back_recv.at[j - 1],
            device_id=(dp_me, peer),
            device_id_type=MESH,
        )
        copy.start()
        back_copies.append(copy)
    own_back = pltpu.make_async_copy(
        result.at[:, my_rows, :], back_ref.at[pl.ds(mp_me * pairs, pairs)], local_sem.at[2]
    )
    own_back.start()

    def find(c, carry):
        def from_source(source, state):
            slot, code = state
            place = source * per_peer
            for f in range(factors):
                hit = table_ref[0, source * factors + f] == dp_me
                code = jnp.where(jnp.logical_and(hit, slot == c), place, code)
                slot = slot + hit.astype(jnp.int32)
                place = place + hit.astype(jnp.int32)
            return slot, code

        codes_ref[0, c] = lax.fori_loop(
            0, dp_count, from_source, (jnp.int32(0), jnp.int32(-1))
        )[1]
        return carry

    lax.fori_loop(0, 2 * factors, find, 0)

    own_back.wait()
    own_roots.wait()
    for copy in back_copies:
        copy.wait()

    def finish(s, carry):
        send(s).wait()
        return carry

    lax.fori_loop(0, dp_count - 1, finish, 0)


def store_kernel(
    per_peer,
    per_step,
    codes_ref,
    recv_ref,
    back_ref,
    store_ref,
    update_ref,
    update_sem,
):
    step = pl.program_id(0)
    half = store_ref.shape[2] // 2
    update_copy = pltpu.make_async_copy(back_ref, update_ref, update_sem)

    @pl.when(step == 0)
    def _():
        update_copy.start()

    down = lax.broadcasted_iota(jnp.int32, (half, half), 0)
    across = lax.broadcasted_iota(jnp.int32, (half, half), 1)
    body = per_peer * 2 * half
    tail = recv_ref.shape[1] - body
    tail_row = lax.broadcasted_iota(jnp.int32, (tail, half), 0)
    for i in range(per_step):
        code = codes_ref[0, step * per_step + i]
        taken = code >= 0
        source = jnp.maximum(code, 0) // per_peer
        place = jnp.maximum(code, 0) % per_peer
        first = pl.multiple_of(place * 2 * half, 2 * half)
        cross = recv_ref[source, pl.ds(first, half), :]
        mixed = recv_ref[source, pl.ds(pl.multiple_of(first + half, half), half), :]
        corners = recv_ref[source, pl.ds(body, tail), :]
        cross = jnp.where(taken, cross, 0.0)
        mixed = jnp.where(taken, mixed, 0.0)
        chosen = jnp.logical_and(tail_row == place, taken)
        corner = jnp.sum(jnp.where(chosen, corners, 0.0), axis=0, keepdims=True)
        turned = mixed.T
        store_ref[i, :half, :half] = jnp.where(down >= across, mixed, turned)
        store_ref[i, :half, half:] = cross.T
        store_ref[i, half:, :half] = cross
        store_ref[i, half:, half:] = jnp.where(
            down < across, mixed, jnp.where(down == across, corner, turned)
        )

    @pl.when(step == pl.num_programs(0) - 1)
    def _():
        update_copy.wait()


def on_device(statistics, gradient, root_table):
    dp_count = lax.axis_size("dp")
    mp_count = lax.axis_size("mp")
    factors, width = statistics.shape[0], statistics.shape[1]
    half, pairs = width // 2, factors // 2
    capacity = 2 * factors
    per_peer = (capacity + dp_count - 1) // dp_count
    length = per_peer * width + (per_peer + 7) // 8 * 8
    smem_spec = pl.BlockSpec(memory_space=pltpu.SMEM)
    any_spec = pl.BlockSpec(memory_space=pl.ANY)
    vmem_spec = pl.BlockSpec(memory_space=pltpu.VMEM)
    hbm_spec = pl.BlockSpec(memory_space=pltpu.HBM)
    received, back, codes = pl.pallas_call(
        functools.partial(spread_kernel, dp_count, mp_count, per_peer),
        out_shape=(
            jax.ShapeDtypeStruct((dp_count, length, half), F32),
            jax.ShapeDtypeStruct(gradient.shape, F32),
            jax.ShapeDtypeStruct((1, capacity), jnp.int32),
        ),
        in_specs=[smem_spec, hbm_spec, hbm_spec],
        out_specs=(any_spec, any_spec, smem_spec),
        scratch_shapes=[
            pltpu.VMEM((factors, width, width), F32),
            pltpu.VMEM((factors, width, width), F32),
            pltpu.VMEM((factors, width, half), F32),
            pltpu.VMEM((factors, 8, half), F32),
            pltpu.VMEM((dp_count, length, half), F32),
            pltpu.VMEM((pairs, width, width), F32),
            pltpu.VMEM((pairs, width, width), F32),
            pltpu.SMEM((factors,), jnp.int32),
            pltpu.SMEM((factors,), jnp.int32),
            pltpu.SMEM((dp_count,), jnp.int32),
            pltpu.SemaphoreType.DMA((mp_count - 1,)),
            pltpu.SemaphoreType.DMA((mp_count - 1,)),
            pltpu.SemaphoreType.DMA((mp_count - 1,)),
            pltpu.SemaphoreType.DMA((mp_count - 1,)),
            pltpu.SemaphoreType.DMA((dp_count - 1,)),
            pltpu.SemaphoreType.DMA((dp_count - 1,)),
            pltpu.SemaphoreType.DMA((4,)),
        ],
        compiler_params=pltpu.CompilerParams(
            collective_id=0, has_side_effects=True, vmem_limit_bytes=28 * 2**20
        ),
    )(root_table, statistics, gradient)
    per_step = 2
    return pl.pallas_call(
        functools.partial(store_kernel, per_peer, per_step),
        grid=(capacity // per_step,),
        out_shape=(
            jax.ShapeDtypeStruct((capacity, width, width), F32),
            jax.ShapeDtypeStruct(gradient.shape, F32),
        ),
        in_specs=[smem_spec, vmem_spec, any_spec],
        out_specs=(pl.BlockSpec((per_step, width, width), lambda s: (s, 0, 0)), any_spec),
        scratch_shapes=[pltpu.SemaphoreType.DMA],
        compiler_params=pltpu.CompilerParams(vmem_limit_bytes=16 * 2**20),
    )(codes, received, back)


def solution(mesh):
    return jax.shard_map(
        on_device,
        mesh=mesh,
        in_specs=(P(("dp", "mp"), None, None), P("dp", "mp", None), P("mp", None)),
        out_specs=(P(("dp", "mp"), None, None), P("dp", "mp", None)),
        check_vma=False,
    )
```

```python
import functools

import jax
import jax.numpy as jnp
from jax import lax
from jax.experimental import pallas as pl
from jax.experimental.pallas import tpu as pltpu
from jax.sharding import PartitionSpec as P

MESH = pl.DeviceIdType.MESH
F32 = jnp.float32
BF16 = jnp.bfloat16


def one_pass(left, right):
    return jnp.dot(left.astype(BF16), right.astype(BF16), preferred_element_type=F32)


def halves(value):
    high = value.astype(BF16)
    return high, (value - high.astype(F32)).astype(BF16)


def three_pass(left, right):
    left_high, left_low = halves(left)
    right_high, right_low = halves(right)
    dot = functools.partial(jnp.dot, preferred_element_type=F32)
    return dot(left_high, right_high) + (dot(left_high, right_low) + dot(left_low, right_high))


def inverse_root(stat, eye_mask):
    scale = jnp.sqrt(jnp.sum(stat * stat, keepdims=True) + 1e-06)
    quarter = 1.0 / jnp.sqrt(jnp.sqrt(scale))
    x = stat * (-0.25 / scale)
    c = 1.5625
    xx = one_pass(x, x)
    a = 2.5 * x + xx
    b = 3.125 * a + one_pass(a, a)
    d = 1.25 * x + xx
    y = 1.25 * x + (c * c) * d + one_pass(b, d)
    z = (2 * c) * y + one_pass(y, y)
    w = (2 * c * c) * z + one_pass(z, z)
    t = c * x + one_pass(x, y)
    e = 1.25 * y + (c**4) * t + three_pass(w, t)
    return quarter * jnp.where(eye_mask, e + 1.25 * c, e)


def flipped(me, mask, count):
    peer = me
    bit = 1
    while bit < count:
        peer = peer + (mask // bit % 2) * (1 - 2 * (me // bit % 2)) * bit
        bit *= 2
    return peer


def nth_mask(s, count):
    if isinstance(s, int) and s == count - 1:
        return 0
    return (1 - s % 2) * (count // 2 + s // 2) + s % 2 * ((s + 1) // 2)


def spread_kernel(
    dp_count,
    mp_count,
    per_peer,
    table_ref,
    stat_ref,
    grad_ref,
    recv_ref,
    back_ref,
    codes_ref,
    stats,
    roots,
    packed,
    corner,
    staged,
    whole,
    result,
    order,
    position,
    bases,
    grad_send,
    grad_recv,
    back_send,
    back_recv,
    out_send,
    out_recv,
    local_sem,
):
    dp_me = lax.axis_index("dp")
    mp_me = lax.axis_index("mp")
    factors, width = stats.shape[0], stats.shape[1]
    half = width // 2
    pairs = factors // 2
    rows = width // mp_count
    stat_copy = pltpu.make_async_copy(stat_ref, stats, local_sem.at[3])
    stat_copy.start()
    my_rows = pl.ds(pl.multiple_of(mp_me * rows, rows), rows)
    own_grad = pltpu.make_async_copy(
        grad_ref.at[pl.ds(mp_me * pairs, pairs)], whole.at[:, my_rows, :], local_sem.at[0]
    )
    own_grad.start()
    barrier = pltpu.get_barrier_semaphore()
    for k in range(1, dp_count):
        pl.semaphore_signal(
            barrier, inc=1, device_id=(lax.rem(dp_me + k, dp_count), mp_me), device_id_type=MESH
        )
    for j in range(1, mp_count):
        pl.semaphore_signal(
            barrier, inc=1, device_id=(dp_me, lax.rem(mp_me + j, mp_count)), device_id_type=MESH
        )

    targets = [table_ref[0, dp_me * factors + f] for f in range(factors)]
    places = [jnp.int32(0)] * factors
    running = jnp.int32(0)
    for s in range(dp_count):
        peer = flipped(dp_me, nth_mask(s, dp_count), dp_count)
        bases[s] = running
        for f in range(factors):
            hit = targets[f] == peer
            places[f] = jnp.where(hit, running, places[f])
            running = running + hit.astype(jnp.int32)
    for f in range(factors):
        position[f] = places[f]
    for i in range(factors):
        which = jnp.int32(0)
        for f in range(factors):
            which = jnp.where(places[f] == i, f, which)
        order[i] = which

    pl.semaphore_wait(barrier, dp_count + mp_count - 2)
    grad_copies = []
    for j in range(1, mp_count):
        peer = lax.rem(mp_me + j, mp_count)
        copy = pltpu.make_async_remote_copy(
            src_ref=grad_ref.at[pl.ds(peer * pairs, pairs)],
            dst_ref=whole.at[:, my_rows, :],
            send_sem=grad_send.at[j - 1],
            recv_sem=grad_recv.at[j - 1],
            device_id=(dp_me, peer),
            device_id_type=MESH,
        )
        copy.start()
        grad_copies.append(copy)

    down = lax.broadcasted_iota(jnp.int32, (half, half), 0)
    across = lax.broadcasted_iota(jnp.int32, (half, half), 1)
    eye_mask = lax.broadcasted_iota(jnp.int32, (width, width), 0) == lax.broadcasted_iota(
        jnp.int32, (width, width), 1
    )
    body = per_peer * width
    tail = staged.shape[1] - body
    tail_row = lax.broadcasted_iota(jnp.int32, (tail, half), 0)

    def stage(s):
        corners = jnp.zeros((tail, half), F32)
        for c in range(per_peer):
            at = jnp.minimum(bases[s] + c, factors - 1)
            staged[s, c * width : (c + 1) * width, :] = packed[at]
            corners = jnp.where(tail_row == c, corner[at][:1], corners)
        staged[s, body:, :] = corners

    def send(s):
        return pltpu.make_async_remote_copy(
            src_ref=staged.at[s],
            dst_ref=recv_ref.at[dp_me],
            send_sem=out_send.at[s],
            recv_sem=out_recv.at[s],
            device_id=(flipped(dp_me, nth_mask(s, dp_count), dp_count), mp_me),
            device_id_type=MESH,
        )

    stat_copy.wait()
    steps = factors // per_peer

    def make_roots(step, carry):
        for i in range(per_peer):
            f = step * per_peer + i
            root = inverse_root(stats[order[f]], eye_mask)
            roots[f] = root
            low = root[half:, half:]
            packed[f, :half, :] = root[half:, :half]
            packed[f, half:, :] = jnp.where(down >= across, root[:half, :half], low)
            diagonal = jnp.sum(jnp.where(down == across, low, 0.0), axis=0, keepdims=True)
            corner[f] = jnp.broadcast_to(diagonal, (8, half))
        stage(step)
        send(step).start()
        return carry

    def send_rest(s, carry):
        stage(s)
        send(s).start()
        return carry

    for f in range(factors):
        packed[f] = jnp.zeros((width, half), F32)
        corner[f] = jnp.zeros((8, half), F32)
    lax.fori_loop(0, steps, make_roots, 0)
    lax.fori_loop(steps, dp_count - 1, send_rest, 0)
    stage(dp_count - 1)
    own_roots = pltpu.make_async_copy(
        staged.at[dp_count - 1], recv_ref.at[dp_me], local_sem.at[1]
    )
    own_roots.start()

    own_grad.wait()
    for copy in grad_copies:
        copy.wait()

    def apply(m, carry):
        left = three_pass(roots[position[2 * m]], whole[m])
        result[m] = three_pass(left, roots[position[2 * m + 1]])
        return carry

    lax.fori_loop(0, pairs, apply, 0)

    back_copies = []
    for j in range(1, mp_count):
        peer = lax.rem(mp_me + j, mp_count)
        copy = pltpu.make_async_remote_copy(
            src_ref=result.at[:, pl.ds(pl.multiple_of(peer * rows, rows), rows), :],
            dst_ref=back_ref.at[pl.ds(mp_me * pairs, pairs)],
            send_sem=back_send.at[j - 1],
            recv_sem=back_recv.at[j - 1],
            device_id=(dp_me, peer),
            device_id_type=MESH,
        )
        copy.start()
        back_copies.append(copy)
    own_back = pltpu.make_async_copy(
        result.at[:, my_rows, :], back_ref.at[pl.ds(mp_me * pairs, pairs)], local_sem.at[2]
    )
    own_back.start()

    def find(c, carry):
        def from_source(source, state):
            slot, code = state
            place = source * per_peer
            for f in range(factors):
                hit = table_ref[0, source * factors + f] == dp_me
                code = jnp.where(jnp.logical_and(hit, slot == c), place, code)
                slot = slot + hit.astype(jnp.int32)
                place = place + hit.astype(jnp.int32)
            return slot, code

        codes_ref[0, c] = lax.fori_loop(
            0, dp_count, from_source, (jnp.int32(0), jnp.int32(-1))
        )[1]
        return carry

    lax.fori_loop(0, 2 * factors, find, 0)

    own_back.wait()
    own_roots.wait()
    for copy in back_copies:
        copy.wait()

    def finish(s, carry):
        send(s).wait()
        return carry

    lax.fori_loop(0, dp_count - 1, finish, 0)


def store_kernel(
    per_peer,
    per_step,
    codes_ref,
    recv_ref,
    back_ref,
    store_ref,
    update_ref,
    update_sem,
):
    step = pl.program_id(0)
    half = store_ref.shape[2] // 2
    update_copy = pltpu.make_async_copy(back_ref, update_ref, update_sem)

    @pl.when(step == 0)
    def _():
        update_copy.start()

    down = lax.broadcasted_iota(jnp.int32, (half, half), 0)
    across = lax.broadcasted_iota(jnp.int32, (half, half), 1)
    body = per_peer * 2 * half
    tail = recv_ref.shape[1] - body
    tail_row = lax.broadcasted_iota(jnp.int32, (tail, half), 0)
    for i in range(per_step):
        code = codes_ref[0, step * per_step + i]
        taken = code >= 0
        source = jnp.maximum(code, 0) // per_peer
        place = jnp.maximum(code, 0) % per_peer
        first = pl.multiple_of(place * 2 * half, 2 * half)
        cross = recv_ref[source, pl.ds(first, half), :]
        mixed = recv_ref[source, pl.ds(pl.multiple_of(first + half, half), half), :]
        corners = recv_ref[source, pl.ds(body, tail), :]
        cross = jnp.where(taken, cross, 0.0)
        mixed = jnp.where(taken, mixed, 0.0)
        chosen = jnp.logical_and(tail_row == place, taken)
        corner = jnp.sum(jnp.where(chosen, corners, 0.0), axis=0, keepdims=True)
        turned = mixed.T
        store_ref[i, :half, :half] = jnp.where(down >= across, mixed, turned)
        store_ref[i, :half, half:] = cross.T
        store_ref[i, half:, :half] = cross
        store_ref[i, half:, half:] = jnp.where(
            down < across, mixed, jnp.where(down == across, corner, turned)
        )

    @pl.when(step == pl.num_programs(0) - 1)
    def _():
        update_copy.wait()


def on_device(statistics, gradient, root_table):
    dp_count = lax.axis_size("dp")
    mp_count = lax.axis_size("mp")
    factors, width = statistics.shape[0], statistics.shape[1]
    half, pairs = width // 2, factors // 2
    capacity = 2 * factors
    per_peer = (capacity + dp_count - 1) // dp_count
    length = per_peer * width + (per_peer + 7) // 8 * 8
    smem_spec = pl.BlockSpec(memory_space=pltpu.SMEM)
    any_spec = pl.BlockSpec(memory_space=pl.ANY)
    vmem_spec = pl.BlockSpec(memory_space=pltpu.VMEM)
    hbm_spec = pl.BlockSpec(memory_space=pltpu.HBM)
    received, back, codes = pl.pallas_call(
        functools.partial(spread_kernel, dp_count, mp_count, per_peer),
        out_shape=(
            jax.ShapeDtypeStruct((dp_count, length, half), F32),
            jax.ShapeDtypeStruct(gradient.shape, F32),
            jax.ShapeDtypeStruct((1, capacity), jnp.int32),
        ),
        in_specs=[smem_spec, hbm_spec, hbm_spec],
        out_specs=(any_spec, any_spec, smem_spec),
        scratch_shapes=[
            pltpu.VMEM((factors, width, width), F32),
            pltpu.VMEM((factors, width, width), F32),
            pltpu.VMEM((factors, width, half), F32),
            pltpu.VMEM((factors, 8, half), F32),
            pltpu.VMEM((dp_count, length, half), F32),
            pltpu.VMEM((pairs, width, width), F32),
            pltpu.VMEM((pairs, width, width), F32),
            pltpu.SMEM((factors,), jnp.int32),
            pltpu.SMEM((factors,), jnp.int32),
            pltpu.SMEM((dp_count,), jnp.int32),
            pltpu.SemaphoreType.DMA((mp_count - 1,)),
            pltpu.SemaphoreType.DMA((mp_count - 1,)),
            pltpu.SemaphoreType.DMA((mp_count - 1,)),
            pltpu.SemaphoreType.DMA((mp_count - 1,)),
            pltpu.SemaphoreType.DMA((dp_count - 1,)),
            pltpu.SemaphoreType.DMA((dp_count - 1,)),
            pltpu.SemaphoreType.DMA((4,)),
        ],
        compiler_params=pltpu.CompilerParams(
            collective_id=0, has_side_effects=True, vmem_limit_bytes=28 * 2**20
        ),
    )(*(pltpu.with_memory_space_constraint(x, pltpu.HBM) for x in (root_table, statistics, gradient)))
    per_step = 2
    return pl.pallas_call(
        functools.partial(store_kernel, per_peer, per_step),
        grid=(capacity // per_step,),
        out_shape=(
            jax.ShapeDtypeStruct((capacity, width, width), F32),
            jax.ShapeDtypeStruct(gradient.shape, F32),
        ),
        in_specs=[smem_spec, vmem_spec, any_spec],
        out_specs=(pl.BlockSpec((per_step, width, width), lambda s: (s, 0, 0)), any_spec),
        scratch_shapes=[pltpu.SemaphoreType.DMA],
        compiler_params=pltpu.CompilerParams(vmem_limit_bytes=16 * 2**20),
    )(codes, received, back)


def solution(mesh):
    return jax.shard_map(
        on_device,
        mesh=mesh,
        in_specs=(P(("dp", "mp"), None, None), P("dp", "mp", None), P("mp", None)),
        out_specs=(P(("dp", "mp"), None, None), P("dp", "mp", None)),
        check_vma=False,
    )
```

```python
import functools

import jax
import jax.numpy as jnp
from jax import lax
from jax.experimental import pallas as pl
from jax.experimental.pallas import tpu as pltpu
from jax.sharding import PartitionSpec as P

MESH = pl.DeviceIdType.MESH
F32 = jnp.float32
BF16 = jnp.bfloat16


def one_pass(left, right):
    return jnp.dot(left.astype(BF16), right.astype(BF16), preferred_element_type=F32)


def halves(value):
    high = value.astype(BF16)
    return high, (value - high.astype(F32)).astype(BF16)


def three_pass(left, right):
    left_high, left_low = halves(left)
    right_high, right_low = halves(right)
    dot = functools.partial(jnp.dot, preferred_element_type=F32)
    return dot(left_high, right_high) + (dot(left_high, right_low) + dot(left_low, right_high))


def inverse_root(stat, eye_mask):
    scale = jnp.sqrt(jnp.sum(stat * stat, keepdims=True) + 1e-06)
    quarter = 1.0 / jnp.sqrt(jnp.sqrt(scale))
    x = stat * (-0.25 / scale)
    c = 1.5625
    xx = one_pass(x, x)
    a = 2.5 * x + xx
    b = 3.125 * a + one_pass(a, a)
    d = 1.25 * x + xx
    y = 1.25 * x + (c * c) * d + one_pass(b, d)
    z = (2 * c) * y + one_pass(y, y)
    w = (2 * c * c) * z + one_pass(z, z)
    t = c * x + one_pass(x, y)
    e = 1.25 * y + (c**4) * t + three_pass(w, t)
    return quarter * jnp.where(eye_mask, e + 1.25 * c, e)


def flipped(me, mask, count):
    peer = me
    bit = 1
    while bit < count:
        peer = peer + (mask // bit % 2) * (1 - 2 * (me // bit % 2)) * bit
        bit *= 2
    return peer


def nth_mask(s, count):
    if isinstance(s, int) and s == count - 1:
        return 0
    return (1 - s % 2) * (count // 2 + s // 2) + s % 2 * ((s + 1) // 2)


def spread_kernel(
    dp_count,
    mp_count,
    per_peer,
    table_ref,
    stat_ref,
    grad_ref,
    recv_ref,
    back_ref,
    codes_ref,
    stats,
    roots,
    packed,
    corner,
    staged,
    whole,
    result,
    order,
    position,
    bases,
    grad_send,
    grad_recv,
    back_send,
    back_recv,
    out_send,
    out_recv,
    local_sem,
):
    dp_me = lax.axis_index("dp")
    mp_me = lax.axis_index("mp")
    factors, width = stats.shape[0], stats.shape[1]
    half = width // 2
    pairs = factors // 2
    rows = width // mp_count
    stat_copy = pltpu.make_async_copy(stat_ref, stats, local_sem.at[3])
    stat_copy.start()
    my_rows = pl.ds(pl.multiple_of(mp_me * rows, rows), rows)
    own_grad = pltpu.make_async_copy(
        grad_ref.at[pl.ds(mp_me * pairs, pairs)], whole.at[:, my_rows, :], local_sem.at[0]
    )
    own_grad.start()
    barrier = pltpu.get_barrier_semaphore()
    for k in range(1, dp_count):
        pl.semaphore_signal(
            barrier, inc=1, device_id=(lax.rem(dp_me + k, dp_count), mp_me), device_id_type=MESH
        )
    for j in range(1, mp_count):
        pl.semaphore_signal(
            barrier, inc=1, device_id=(dp_me, lax.rem(mp_me + j, mp_count)), device_id_type=MESH
        )

    targets = [table_ref[0, dp_me * factors + f] for f in range(factors)]
    places = [jnp.int32(0)] * factors
    running = jnp.int32(0)
    for s in range(dp_count):
        peer = flipped(dp_me, nth_mask(s, dp_count), dp_count)
        bases[s] = running
        for f in range(factors):
            hit = targets[f] == peer
            places[f] = jnp.where(hit, running, places[f])
            running = running + hit.astype(jnp.int32)
    for f in range(factors):
        position[f] = places[f]
    for i in range(factors):
        which = jnp.int32(0)
        for f in range(factors):
            which = jnp.where(places[f] == i, f, which)
        order[i] = which

    pl.semaphore_wait(barrier, dp_count + mp_count - 2)
    grad_copies = []
    for j in range(1, mp_count):
        peer = lax.rem(mp_me + j, mp_count)
        copy = pltpu.make_async_remote_copy(
            src_ref=grad_ref.at[pl.ds(peer * pairs, pairs)],
            dst_ref=whole.at[:, my_rows, :],
            send_sem=grad_send.at[j - 1],
            recv_sem=grad_recv.at[j - 1],
            device_id=(dp_me, peer),
            device_id_type=MESH,
        )
        copy.start()
        grad_copies.append(copy)

    down = lax.broadcasted_iota(jnp.int32, (half, half), 0)
    across = lax.broadcasted_iota(jnp.int32, (half, half), 1)
    eye_mask = lax.broadcasted_iota(jnp.int32, (width, width), 0) == lax.broadcasted_iota(
        jnp.int32, (width, width), 1
    )
    body = per_peer * width
    tail = staged.shape[1] - body
    tail_row = lax.broadcasted_iota(jnp.int32, (tail, half), 0)

    def stage(s):
        corners = jnp.zeros((tail, half), F32)
        for c in range(per_peer):
            at = jnp.minimum(bases[s] + c, factors - 1)
            staged[s, c * width : (c + 1) * width, :] = packed[at]
            corners = jnp.where(tail_row == c, corner[at][:1], corners)
        staged[s, body:, :] = corners

    def send(s):
        return pltpu.make_async_remote_copy(
            src_ref=staged.at[s],
            dst_ref=recv_ref.at[dp_me],
            send_sem=out_send.at[s],
            recv_sem=out_recv.at[s],
            device_id=(flipped(dp_me, nth_mask(s, dp_count), dp_count), mp_me),
            device_id_type=MESH,
        )

    stat_copy.wait()
    steps = factors // per_peer

    def make_roots(step, carry):
        for i in range(per_peer):
            f = step * per_peer + i
            root = inverse_root(stats[order[f]], eye_mask)
            roots[f] = root
            low = root[half:, half:]
            packed[f, :half, :] = root[half:, :half]
            packed[f, half:, :] = jnp.where(down >= across, root[:half, :half], low)
            diagonal = jnp.sum(jnp.where(down == across, low, 0.0), axis=0, keepdims=True)
            corner[f] = jnp.broadcast_to(diagonal, (8, half))
        stage(step)
        send(step).start()
        return carry

    def send_rest(s, carry):
        stage(s)
        send(s).start()
        return carry

    for f in range(factors):
        packed[f] = jnp.zeros((width, half), F32)
        corner[f] = jnp.zeros((8, half), F32)
    lax.fori_loop(0, steps, make_roots, 0)
    lax.fori_loop(steps, dp_count - 1, send_rest, 0)
    stage(dp_count - 1)
    own_roots = pltpu.make_async_copy(
        staged.at[dp_count - 1], recv_ref.at[dp_me], local_sem.at[1]
    )
    own_roots.start()

    own_grad.wait()
    for copy in grad_copies:
        copy.wait()

    def apply(m, carry):
        left = three_pass(roots[position[2 * m]], whole[m])
        result[m] = three_pass(left, roots[position[2 * m + 1]])
        return carry

    lax.fori_loop(0, pairs, apply, 0)

    back_copies = []
    for j in range(1, mp_count):
        peer = lax.rem(mp_me + j, mp_count)
        copy = pltpu.make_async_remote_copy(
            src_ref=result.at[:, pl.ds(pl.multiple_of(peer * rows, rows), rows), :],
            dst_ref=back_ref.at[pl.ds(mp_me * pairs, pairs)],
            send_sem=back_send.at[j - 1],
            recv_sem=back_recv.at[j - 1],
            device_id=(dp_me, peer),
            device_id_type=MESH,
        )
        copy.start()
        back_copies.append(copy)
    own_back = pltpu.make_async_copy(
        result.at[:, my_rows, :], back_ref.at[pl.ds(mp_me * pairs, pairs)], local_sem.at[2]
    )
    own_back.start()

    def find(c, carry):
        def from_source(source, state):
            slot, code = state
            place = source * per_peer
            for f in range(factors):
                hit = table_ref[0, source * factors + f] == dp_me
                code = jnp.where(jnp.logical_and(hit, slot == c), place, code)
                slot = slot + hit.astype(jnp.int32)
                place = place + hit.astype(jnp.int32)
            return slot, code

        codes_ref[0, c] = lax.fori_loop(
            0, dp_count, from_source, (jnp.int32(0), jnp.int32(-1))
        )[1]
        return carry

    lax.fori_loop(0, 2 * factors, find, 0)

    own_back.wait()
    own_roots.wait()
    for copy in back_copies:
        copy.wait()

    def finish(s, carry):
        send(s).wait()
        return carry

    lax.fori_loop(0, dp_count - 1, finish, 0)


def store_kernel(
    per_peer,
    per_step,
    codes_ref,
    recv_ref,
    back_ref,
    store_ref,
    update_ref,
    update_sem,
):
    step = pl.program_id(0)
    half = store_ref.shape[2] // 2
    update_copy = pltpu.make_async_copy(back_ref, update_ref, update_sem)

    @pl.when(step == 0)
    def _():
        update_copy.start()

    down = lax.broadcasted_iota(jnp.int32, (half, half), 0)
    across = lax.broadcasted_iota(jnp.int32, (half, half), 1)
    body = per_peer * 2 * half
    tail = recv_ref.shape[1] - body
    tail_row = lax.broadcasted_iota(jnp.int32, (tail, half), 0)
    for i in range(per_step):
        code = codes_ref[0, step * per_step + i]
        taken = code >= 0
        source = jnp.maximum(code, 0) // per_peer
        place = jnp.maximum(code, 0) % per_peer
        first = pl.multiple_of(place * 2 * half, 2 * half)
        cross = recv_ref[source, pl.ds(first, half), :]
        mixed = recv_ref[source, pl.ds(pl.multiple_of(first + half, half), half), :]
        corners = recv_ref[source, pl.ds(body, tail), :]
        cross = jnp.where(taken, cross, 0.0)
        mixed = jnp.where(taken, mixed, 0.0)
        chosen = jnp.logical_and(tail_row == place, taken)
        corner = jnp.sum(jnp.where(chosen, corners, 0.0), axis=0, keepdims=True)
        turned = mixed.T
        store_ref[i, :half, :half] = jnp.where(down >= across, mixed, turned)
        store_ref[i, :half, half:] = cross.T
        store_ref[i, half:, :half] = cross
        store_ref[i, half:, half:] = jnp.where(
            down < across, mixed, jnp.where(down == across, corner, turned)
        )

    @pl.when(step == pl.num_programs(0) - 1)
    def _():
        update_copy.wait()


def on_device(statistics, gradient, root_table):
    dp_count = lax.axis_size("dp")
    mp_count = lax.axis_size("mp")
    factors, width = statistics.shape[0], statistics.shape[1]
    half, pairs = width // 2, factors // 2
    capacity = 2 * factors
    per_peer = (capacity + dp_count - 1) // dp_count
    length = per_peer * width + (per_peer + 7) // 8 * 8
    smem_spec = pl.BlockSpec(memory_space=pltpu.SMEM)
    any_spec = pl.BlockSpec(memory_space=pl.ANY)
    vmem_spec = pl.BlockSpec(memory_space=pltpu.VMEM)
    hbm_spec = pl.BlockSpec(memory_space=pltpu.HBM)
    received, back, codes = pl.pallas_call(
        functools.partial(spread_kernel, dp_count, mp_count, per_peer),
        out_shape=(
            jax.ShapeDtypeStruct((dp_count, length, half), F32),
            jax.ShapeDtypeStruct(gradient.shape, F32),
            jax.ShapeDtypeStruct((1, capacity), jnp.int32),
        ),
        in_specs=[smem_spec, hbm_spec, hbm_spec],
        out_specs=(any_spec, any_spec, smem_spec),
        scratch_shapes=[
            pltpu.VMEM((factors, width, width), F32),
            pltpu.VMEM((factors, width, width), F32),
            pltpu.VMEM((factors, width, half), F32),
            pltpu.VMEM((factors, 8, half), F32),
            pltpu.VMEM((dp_count, length, half), F32),
            pltpu.VMEM((pairs, width, width), F32),
            pltpu.VMEM((pairs, width, width), F32),
            pltpu.SMEM((factors,), jnp.int32),
            pltpu.SMEM((factors,), jnp.int32),
            pltpu.SMEM((dp_count,), jnp.int32),
            pltpu.SemaphoreType.DMA((mp_count - 1,)),
            pltpu.SemaphoreType.DMA((mp_count - 1,)),
            pltpu.SemaphoreType.DMA((mp_count - 1,)),
            pltpu.SemaphoreType.DMA((mp_count - 1,)),
            pltpu.SemaphoreType.DMA((dp_count - 1,)),
            pltpu.SemaphoreType.DMA((dp_count - 1,)),
            pltpu.SemaphoreType.DMA((4,)),
        ],
        compiler_params=pltpu.CompilerParams(
            collective_id=0, has_side_effects=True, vmem_limit_bytes=28 * 2**20
        ),
    )(*(pltpu.with_memory_space_constraint(x, pltpu.HBM) for x in (root_table, statistics, gradient)))
    per_step = 4
    return pl.pallas_call(
        functools.partial(store_kernel, per_peer, per_step),
        grid=(capacity // per_step,),
        out_shape=(
            jax.ShapeDtypeStruct((capacity, width, width), F32),
            jax.ShapeDtypeStruct(gradient.shape, F32),
        ),
        in_specs=[smem_spec, vmem_spec, any_spec],
        out_specs=(pl.BlockSpec((per_step, width, width), lambda s: (s, 0, 0)), any_spec),
        scratch_shapes=[pltpu.SemaphoreType.DMA],
        compiler_params=pltpu.CompilerParams(vmem_limit_bytes=16 * 2**20),
    )(codes, received, back)


def solution(mesh):
    return jax.shard_map(
        on_device,
        mesh=mesh,
        in_specs=(P(("dp", "mp"), None, None), P("dp", "mp", None), P("mp", None)),
        out_specs=(P(("dp", "mp"), None, None), P("dp", "mp", None)),
        check_vma=False,
    )
```
